32 devices in a mesh: section: 4 (over z), ctx: 2 (over x), tp: 4 (over y, core).
Axes of the slice: x: 2, y: 2, z: 4, core: 2. Of those that a mesh axis runs over, the one named last changes fastest.
Arguments:
- block_order: int32 [4], replicated, may hold values from 0 to 3, each once
- plan: int32 [4], replicated, may hold values from 0 to 1
- q_box: bfloat16 [4, 2, 352, 8192], P('section', None, 'ctx', 'tp'), may hold values from -8 to 8
- k_box: bfloat16 [4, 2, 352, 1024], P('section', None, ('ctx', 'tp')), may hold values from -8 to 8
- v_box: bfloat16 [4, 2, 352, 1024], P('section', None, ('ctx', 'tp')), may hold values from -6 to 6
- grad_out: bfloat16 [4, 352, 8192], P('section', 'ctx', 'tp'), may hold values from -6 to 6
Outputs:
- attn_out: bfloat16 [4, 352, 8192], P('section', 'ctx', 'tp')
- grad_q: bfloat16 [4, 352, 8192], P('section', 'ctx', 'tp')
- grad_k: float32 [4, 352, 1024], P('section', ('ctx', 'tp'))
- grad_v: float32 [4, 352, 1024], P('section', ('ctx', 'tp'))
The draws below stay inside these ranges and needn't reach their ends.
Inputs may be any that keep to these rules, and one draw needn't show every extreme that they name: `block_order`: a permutation: every block sits in exactly one storage slot, slot j covering storage rows j * 88 to (j + 1) * 88 - 1.
All inputs are finite; a program needn't handle non-finite values.
Results may differ from the reference program's by a relative error of at most 0.012.
Values may be sent and summed in bfloat16 or wider, within the bound.
A program may use at most 64 MiB of HBM per device.

```python
import jax
import jax.numpy as jnp
from jax import lax

HEADS = 64
KV_HEADS = 8
HEAD_DIM = 128
MB = 2
SECTIONS = 4
L = 352
BLOCK = 88
NCHUNK = 4
QW = 8192
KW = 1024


def base_values(key, width):
    shape = (SECTIONS, MB, L, width)
    values = jax.random.normal(jax.random.fold_in(key, 13), shape, jnp.float32)
    return jnp.clip(values, -6.0, 6.0)


def draw_q_box(key, part):
    values = base_values(jax.random.fold_in(key, 21), QW)
    return values.astype(jnp.bfloat16)


def draw_k_box(key, part):
    values = base_values(jax.random.fold_in(key, 31), KW)
    return jnp.clip(values, -8.0, 8.0).astype(jnp.bfloat16)


def with_ends(result, stream_key, low, high):
    dims = result.shape
    index_at = [jax.random.randint(jax.random.fold_in(stream_key, axis), (), 0, dims[axis]) for axis in range(len(dims))]
    result = result.at[tuple(index_at)].set(low)
    longest = dims.index(max(dims))
    index_at[longest] = (index_at[longest] + 1) % dims[longest]
    return result.at[tuple(index_at)].set(high)


def block_scale(key, extent, pieces, least, top_value):
    level, own = 1.0, jax.random.fold_in(key, 6)
    for axis_at, blocks in pieces:
        heights = jnp.exp(jax.random.uniform(jax.random.fold_in(own, axis_at), (blocks,), jnp.float32, least / len(pieces), top_value / len(pieces)))
        level = level * jnp.repeat(heights, extent[axis_at] // blocks).reshape([-1 if axis == axis_at else 1 for axis in range(len(extent))])
    return level


def normal_values(stream_key, shape, spread, limit, pieces=(), held_as=jnp.bfloat16):
    entries = jax.random.normal(stream_key, shape, jnp.float32) * spread
    if len(pieces) > 0:
        entries = block_scale(stream_key, shape, pieces, -0.22, 0.18) * entries
    return jnp.clip(entries, min=-limit, max=limit).astype(held_as)


def setup_inputs(seed: int = 0) -> dict:
    streams_of = jax.random.split(jax.random.key(seed), 7)
    block_order = jax.random.permutation(streams_of[0], NCHUNK).astype(jnp.int32)
    plan = with_ends(jax.random.randint(streams_of[1], (SECTIONS,), 0, MB), jax.random.fold_in(streams_of[1], 1), 0, MB - 1).astype(jnp.int32)
    q_box = draw_q_box(jax.random.fold_in(streams_of[6], 71), 0)
    k_box = draw_k_box(jax.random.fold_in(streams_of[6], 71), 0)
    v_box = normal_values(streams_of[4], (SECTIONS, MB, L, KW), 1.0, 6.0, ((0, 4), (2, 8)))
    grad_out = normal_values(streams_of[5], (SECTIONS, L, QW), 1.0, 6.0, ((0, 4), (1, 2), (2, 4)))
    return {"block_order": block_order, "plan": plan, "q_box": q_box, "k_box": k_box, "v_box": v_box, "grad_out": grad_out}


NEG = -1e30


def head_grads(q_head, k_head, v_head, do_head, visible):
    scale = HEAD_DIM ** -0.5
    scores = jnp.dot(q_head, k_head.T, preferred_element_type=jnp.float32) * scale
    scores = jnp.where(visible, scores, NEG)
    top_score = jnp.max(scores, axis=1, keepdims=True)
    totals = jnp.sum(jnp.where(visible, jnp.exp(scores - top_score), 0.0), axis=1, keepdims=True)
    log_total = top_score + jnp.log(totals)
    probs = jnp.where(visible, jnp.exp(scores - log_total), 0.0)
    probs_low = probs.astype(jnp.bfloat16)
    attended = jnp.dot(probs_low, v_head, preferred_element_type=jnp.float32)
    delta = jnp.sum(do_head.astype(jnp.float32) * attended, axis=1, keepdims=True)
    dprobs = jnp.dot(do_head, v_head.T, preferred_element_type=jnp.float32)
    dscores = (probs * (dprobs - delta)).astype(jnp.bfloat16)
    q_grad = (jnp.dot(dscores, k_head, preferred_element_type=jnp.float32) * scale).astype(jnp.bfloat16)
    k_grad = jnp.dot(dscores.T, q_head, preferred_element_type=jnp.float32) * scale
    v_grad = jnp.dot(probs_low.T, do_head, preferred_element_type=jnp.float32)
    return attended.astype(jnp.bfloat16), q_grad, k_grad, v_grad


def reference(block_order, plan, q_box, k_box, v_box, grad_out):
    positions = (block_order[:, None] * BLOCK + jnp.arange(BLOCK, dtype=jnp.int32)[None, :]).reshape(L)
    visible = positions[None, :] <= positions[:, None]
    group = HEADS // KV_HEADS
    outputs = []
    grads_q = []
    grads_k = []
    grads_v = []
    for section in range(SECTIONS):
        source = (section - 1) % SECTIONS
        target = (section + 1) % SECTIONS
        picked = plan[section]
        q_all = lax.dynamic_index_in_dim(q_box[source], picked, 0, keepdims=False)
        k_all = lax.dynamic_index_in_dim(k_box[source], picked, 0, keepdims=False)
        v_all = lax.dynamic_index_in_dim(v_box[source], picked, 0, keepdims=False)
        do_all = grad_out[target]
        q_heads = q_all.reshape(L, HEADS, HEAD_DIM).transpose(1, 0, 2)
        do_heads = do_all.reshape(L, HEADS, HEAD_DIM).transpose(1, 0, 2)
        k_heads = k_all.reshape(L, KV_HEADS, HEAD_DIM).transpose(1, 0, 2)
        v_heads = v_all.reshape(L, KV_HEADS, HEAD_DIM).transpose(1, 0, 2)

        def one_head(head_index):
            kv_index = head_index // group
            q_head = lax.dynamic_index_in_dim(q_heads, head_index, 0, keepdims=False)
            do_head = lax.dynamic_index_in_dim(do_heads, head_index, 0, keepdims=False)
            k_head = lax.dynamic_index_in_dim(k_heads, kv_index, 0, keepdims=False)
            v_head = lax.dynamic_index_in_dim(v_heads, kv_index, 0, keepdims=False)
            return head_grads(q_head, k_head, v_head, do_head, visible)

        attended, q_grad, k_grad, v_grad = lax.map(one_head, jnp.arange(HEADS, dtype=jnp.int32))
        outputs.append(attended.transpose(1, 0, 2).reshape(L, QW))
        grads_q.append(q_grad.transpose(1, 0, 2).reshape(L, QW))
        k_sum = jnp.sum(k_grad.reshape(KV_HEADS, group, L, HEAD_DIM), axis=1)
        v_sum = jnp.sum(v_grad.reshape(KV_HEADS, group, L, HEAD_DIM), axis=1)
        grads_k.append(k_sum.transpose(1, 0, 2).reshape(L, KW))
        grads_v.append(v_sum.transpose(1, 0, 2).reshape(L, KW))
    return (jnp.stack(outputs), jnp.stack(grads_q), jnp.stack(grads_k), jnp.stack(grads_v))
```

```python
import functools
import math

import jax
import jax.numpy as jnp
from jax import lax
from jax.experimental import pallas as pl
from jax.experimental.pallas import tpu as pltpu
from jax.sharding import PartitionSpec as P

HEAD_DIM = 128
NEG = -1e30
MESH = pl.DeviceIdType.MESH
F32 = jnp.float32
BF16 = jnp.bfloat16


def nt_dot(a, b):
    return lax.dot_general(a, b, (((1,), (1,)), ((), ())), preferred_element_type=F32)


def tn_dot(a, b):
    return lax.dot_general(a, b, (((0,), (0,)), ((), ())), preferred_element_type=F32)


def kernel(
    dims,
    order_ref, plan_ref, q_hbm, k_hbm, v_hbm, do_hbm,
    attn_hbm, dq_hbm, dk_hbm, dv_hbm,
    q_in, q_send, q_got, do_got, k_in, v_in, kv_send, kv_all, bias,
    attn_buf, dq_buf, dk_acc, dv_acc, g_send, g_got, dk_out, dv_out,
    q_lsem, k_lsem, q_ssem, q_rsem, do_ssem, do_rsem, kv_ssem, kv_rsem, fw_ssem,
    g_ssem, g_rsem, out_sem, grad_sem,
):
    S, C, TP, R, KR, KP, kl, group, CH, block_len = dims
    hd = HEAD_DIM
    W = kl * hd
    NB = C * TP
    KK = NB * KP
    CW = CH * hd
    per_kv = group // CH
    chunks = kl * per_kv
    slots = NB * KR // block_len
    s, c, t = lax.axis_index("section"), lax.axis_index("ctx"), lax.axis_index("tp")
    me = c * TP + t
    after, before = lax.rem(s + 1, S), lax.rem(s + S - 1, S)

    def q_load(i):
        cols = pl.ds(pl.multiple_of(i * CW, CW), CW)
        return pltpu.make_async_copy(q_hbm.at[0, :, :, cols], q_in.at[i], q_lsem.at[i])

    k_load = pltpu.make_async_copy(k_hbm.at[0], k_in, k_lsem.at[0])
    v_load = pltpu.make_async_copy(v_hbm.at[0], v_in, k_lsem.at[1])
    k_load.start()
    v_load.start()
    for i in range(chunks):
        q_load(i).start()

    barrier = pltpu.get_barrier_semaphore()

    @pl.loop(0, TP)
    def _(u):
        pl.semaphore_signal(barrier, inc=1, device_id={"section": after, "ctx": c, "tp": u}, device_id_type=MESH)
        pl.semaphore_signal(barrier, inc=1, device_id={"section": before, "ctx": c, "tp": u}, device_id_type=MESH)

    @pl.loop(1, NB)
    def _(o):
        b = lax.rem(me + o, NB)
        pl.semaphore_signal(barrier, inc=1, device_id={"section": s, "ctx": b // TP, "tp": lax.rem(b, TP)}, device_id_type=MESH)

    def do_copy(i):
        cols = pl.ds(pl.multiple_of(i * CW, CW), CW)
        return pltpu.make_async_remote_copy(
            src_ref=do_hbm.at[0, :, cols], dst_ref=do_got.at[i],
            send_sem=do_ssem.at[i], recv_sem=do_rsem.at[i],
            device_id={"section": before, "ctx": c, "tp": t}, device_id_type=MESH)

    def q_copy(i):
        return pltpu.make_async_remote_copy(
            src_ref=q_send.at[i], dst_ref=q_got.at[i],
            send_sem=q_ssem.at[i], recv_sem=q_rsem.at[i],
            device_id={"section": after, "ctx": c, "tp": t}, device_id_type=MESH)

    def kv_copy(u, b):
        return pltpu.make_async_remote_copy(
            src_ref=kv_send.at[u], dst_ref=kv_all.at[b],
            send_sem=kv_ssem.at[u], recv_sem=kv_rsem.at[b],
            device_id={"section": after, "ctx": c, "tp": u}, device_id_type=MESH)

    def kv_forward(b, u, to):
        return pltpu.make_async_remote_copy(
            src_ref=kv_all.at[b], dst_ref=kv_all.at[b],
            send_sem=fw_ssem.at[u, to], recv_sem=kv_rsem.at[b],
            device_id={"section": s, "ctx": to, "tp": t}, device_id_type=MESH)

    def g_copy(g, to, frm):
        return pltpu.make_async_remote_copy(
            src_ref=g_send.at[g, to], dst_ref=g_got.at[g, frm],
            send_sem=g_ssem.at[g, to], recv_sem=g_rsem.at[g, frm],
            device_id={"section": s, "ctx": to // TP, "tp": lax.rem(to, TP)}, device_id_type=MESH)

    slot = plan_ref[after]

    def picked(options):
        value = options[0]
        for m in range(1, len(options)):
            value = jnp.where(slot == m, options[m], value)
        return value

    k_load.wait()
    v_load.wait()
    for u in range(TP):
        for kind, src in enumerate((k_in, v_in)):
            if KP != KR:
                kv_send[u, kind, KP - 16:, :] = jnp.zeros((16, W), BF16)
            kv_send[u, kind, :KR, :] = picked(
                [src[m, :, u * W:(u + 1) * W] for m in range(src.shape[0])])

    pl.semaphore_wait(barrier, 2 * TP + NB - 1)

    for o in range(TP):
        u = lax.rem(t + o, TP)
        kv_copy(u, me).start()
    for i in range(chunks):
        q_load(i).wait()
        q_send[i] = picked([q_in[i, m] for m in range(q_in.shape[1])])
        q_copy(i).start()
        do_copy(i).start()

    col = lax.broadcasted_iota(jnp.int32, (1, KK), 1)
    blk = col // KP
    inner = col - blk * KP
    store_row = blk * KR + inner
    key_slot = store_row // block_len
    key_pos = store_row - key_slot * block_len
    for j in range(slots):
        key_pos = key_pos + jnp.where(key_slot == j, order_ref[j] * block_len, 0)
    key_pos = jnp.where(inner < KR, key_pos, jnp.int32(2**30))
    row = lax.broadcasted_iota(jnp.int32, (R, 1), 0)
    query_pos = row
    for j in range(R // block_len):
        base = order_ref[c * (R // block_len) + j] * block_len - j * block_len
        query_pos = query_pos + jnp.where(row // block_len == j, base, 0)
    bias[...] = jnp.where(key_pos <= query_pos, 0.0, NEG).astype(F32)

    for o in range(TP):
        u = lax.rem(t + TP - o, TP)
        b = c * TP + u
        kv_copy(t, b).wait_recv()

        @pl.loop(1, C)
        def _(k):
            kv_forward(b, u, lax.rem(c + k, C)).start()

    @pl.loop(TP, NB)
    def _(o):
        b = lax.rem(c * TP + o, NB)
        kv_copy(t, b).wait_recv()

    scale = hd ** -0.5
    scale2 = scale * math.log2(math.e)

    def out_copies(i):
        cols = pl.ds(pl.multiple_of(i * CW, CW), CW)
        return (
            pltpu.make_async_copy(attn_buf.at[i], attn_hbm.at[0, :, cols], out_sem.at[0, i]),
            pltpu.make_async_copy(dq_buf.at[i], dq_hbm.at[0, :, cols], out_sem.at[1, i]),
        )

    for g in range(kl):
        gc = slice(g * hd, (g + 1) * hd)
        dk_acc[...] = jnp.zeros_like(dk_acc)
        dv_acc[...] = jnp.zeros_like(dv_acc)

        @pl.loop(0, per_kv)
        def _(n):
            i = g * per_kv + n
            keys = kv_all[:, 0, :, gc].reshape(KK, hd)
            values = kv_all[:, 1, :, gc].reshape(KK, hd)
            q_copy(i).wait_recv()
            do_copy(i).wait_recv()
            for h in range(CH):
                hc = slice(h * hd, (h + 1) * hd)
                q = q_got[i, :, hc]
                do = do_got[i, :, hc]
                scores = nt_dot(q, keys) * scale2 + bias[...]
                top = jnp.max(scores, axis=1, keepdims=True)
                e = jnp.exp2(scores - top)
                total = jnp.sum(e, axis=1, keepdims=True)
                probs = e * (1.0 / total)
                low = probs.astype(BF16)
                attended = jnp.dot(low, values, preferred_element_type=F32)
                delta = jnp.sum(do.astype(F32) * attended, axis=1, keepdims=True)
                dprobs = nt_dot(do, values)
                ds = (probs * (dprobs - delta)).astype(BF16)
                attn_buf[i, :, hc] = attended.astype(BF16)
                dq_buf[i, :, hc] = (jnp.dot(ds, keys, preferred_element_type=F32) * scale).astype(BF16)
                dk_acc[...] += tn_dot(q, ds)
                dv_acc[...] += tn_dot(do, low)
            for copy in out_copies(i):
                copy.start()

        g_send[g, :, 0] = (dk_acc[...] * scale).T.astype(BF16).reshape(NB, KP, hd)
        g_send[g, :, 1] = dv_acc[...].T.astype(BF16).reshape(NB, KP, hd)

        @pl.loop(1, NB)
        def _(o):
            g_copy(g, lax.rem(me + o, NB), me).start()

        g_got[g, me] = g_send[g, me]

    for g in range(kl):
        @pl.loop(1, NB)
        def _(o):
            g_copy(g, me, lax.rem(me + o, NB)).wait_recv()

        for u in range(TP):
            cols = slice((u * kl + g) * hd, (u * kl + g + 1) * hd)
            for kind, out in enumerate((dk_out, dv_out)):
                total = g_got[g, u, kind].astype(F32)
                for cc in range(1, C):
                    total = total + g_got[g, cc * TP + u, kind].astype(F32)
                out[:, cols] = total[:KR]
    dk_copy = pltpu.make_async_copy(dk_out, dk_hbm.at[0], grad_sem.at[0])
    dv_copy = pltpu.make_async_copy(dv_out, dv_hbm.at[0], grad_sem.at[1])
    dk_copy.start()
    dv_copy.start()

    @pl.loop(0, TP)
    def _(u):
        kv_copy(u, me).wait_send()

        @pl.loop(1, C)
        def _(k):
            kv_forward(c * TP + u, u, lax.rem(c + k, C)).wait_send()

    for g in range(kl):
        @pl.loop(1, NB)
        def _(o):
            g_copy(g, lax.rem(me + o, NB), me).wait_send()

    for i in range(chunks):
        q_copy(i).wait_send()
        do_copy(i).wait_send()
        for copy in out_copies(i):
            copy.wait()
    dk_copy.wait()
    dv_copy.wait()


def solution(mesh):
    S, C, TP = mesh.shape["section"], mesh.shape["ctx"], mesh.shape["tp"]

    def body(block_order, plan, q_box, k_box, v_box, grad_out):
        hd = HEAD_DIM
        R, QC = q_box.shape[2:]
        KR, KW = k_box.shape[2:]
        block_len = R * C // block_order.shape[0]
        kl = KW // hd // TP
        group = QC // hd // kl
        CH = 2
        KP = -(-KR // 16) * 16
        NB = C * TP
        W = kl * hd
        CW = CH * hd
        chunks = QC // CW
        dims = (S, C, TP, R, KR, KP, kl, group, CH, block_len)
        dma = pltpu.SemaphoreType.DMA
        anywhere = pl.BlockSpec(memory_space=pl.ANY)
        smem = pl.BlockSpec(memory_space=pltpu.SMEM)
        return pl.pallas_call(
            functools.partial(kernel, dims),
            out_shape=(
                jax.ShapeDtypeStruct((1, R, QC), BF16),
                jax.ShapeDtypeStruct((1, R, QC), BF16),
                jax.ShapeDtypeStruct((1, KR, KW), F32),
                jax.ShapeDtypeStruct((1, KR, KW), F32),
            ),
            in_specs=[smem, smem] + [anywhere] * 4,
            out_specs=[anywhere] * 4,
            scratch_shapes=[
                pltpu.VMEM((chunks, q_box.shape[1], R, CW), BF16),
                pltpu.VMEM((chunks, R, CW), BF16),
                pltpu.VMEM((chunks, R, CW), BF16),
                pltpu.VMEM((chunks, R, CW), BF16),
                pltpu.VMEM(k_box.shape[1:], BF16),
                pltpu.VMEM(k_box.shape[1:], BF16),
                pltpu.VMEM((TP, 2, KP, W), BF16),
                pltpu.VMEM((NB, 2, KP, W), BF16),
                pltpu.VMEM((R, NB * KP), F32),
                pltpu.VMEM((chunks, R, CW), BF16),
                pltpu.VMEM((chunks, R, CW), BF16),
                pltpu.VMEM((hd, NB * KP), F32),
                pltpu.VMEM((hd, NB * KP), F32),
                pltpu.VMEM((kl, NB, 2, KP, hd), BF16),
                pltpu.VMEM((kl, NB, 2, KP, hd), BF16),
                pltpu.VMEM((KR, KW), F32),
                pltpu.VMEM((KR, KW), F32),
                dma((chunks,)), dma((2,)), dma((chunks,)), dma((chunks,)), dma((chunks,)), dma((chunks,)),
                dma((TP,)), dma((NB,)), dma((TP, C)), dma((kl, NB)), dma((kl, NB)), dma((2, chunks)), dma((2,)),
            ],
            compiler_params=pltpu.CompilerParams(
                collective_id=0, has_side_effects=True, vmem_limit_bytes=40 * 1024 * 1024
            ),
        )(block_order, plan, q_box, k_box, v_box, grad_out)

    in_specs = (
        P(),
        P(),
        P("section", None, "ctx", "tp"),
        P("section", None, ("ctx", "tp"), None),
        P("section", None, ("ctx", "tp"), None),
        P("section", "ctx", "tp"),
    )
    out_specs = (
        P("section", "ctx", "tp"),
        P("section", "ctx", "tp"),
        P("section", ("ctx", "tp"), None),
        P("section", ("ctx", "tp"), None),
    )
    return jax.shard_map(body, mesh=mesh, in_specs=in_specs, out_specs=out_specs, check_vma=False)
```

```python
import functools
import math

import jax
import jax.numpy as jnp
from jax import lax
from jax.experimental import pallas as pl
from jax.experimental.pallas import tpu as pltpu
from jax.sharding import PartitionSpec as P

HEAD_DIM = 128
NEG = -1e30
MESH = pl.DeviceIdType.MESH
F32 = jnp.float32
BF16 = jnp.bfloat16


def nt_dot(a, b):
    return lax.dot_general(a, b, (((1,), (1,)), ((), ())), preferred_element_type=F32)


def tn_dot(a, b):
    return lax.dot_general(a, b, (((0,), (0,)), ((), ())), preferred_element_type=F32)


def kernel(
    dims,
    order_hbm, plan_hbm, q_hbm, k_hbm, v_hbm, do_hbm,
    attn_hbm, dq_hbm, dk_hbm, dv_hbm,
    order_ref, plan_ref, q_in, q_send, q_got, do_got, k_in, v_in, kv_send, kv_all, bias,
    attn_buf, dq_buf, dk_acc, dv_acc, g_send, g_got, dk_out, dv_out,
    q_lsem, k_lsem, q_ssem, q_rsem, do_ssem, do_rsem, kv_ssem, kv_rsem, fw_ssem,
    g_ssem, g_rsem, out_sem, grad_sem,
):
    S, C, TP, R, KR, KP, kl, group, CH, block_len = dims
    hd = HEAD_DIM
    W = kl * hd
    NB = C * TP
    KK = NB * KP
    CW = CH * hd
    per_kv = group // CH
    chunks = kl * per_kv
    slots = NB * KR // block_len
    s, c, t = lax.axis_index("section"), lax.axis_index("ctx"), lax.axis_index("tp")
    me = c * TP + t
    after, before = lax.rem(s + 1, S), lax.rem(s + S - 1, S)

    def q_load(i):
        cols = pl.ds(pl.multiple_of(i * CW, CW), CW)
        return pltpu.make_async_copy(q_hbm.at[0, :, :, cols], q_in.at[i], q_lsem.at[i])

    k_load = pltpu.make_async_copy(k_hbm.at[0], k_in, k_lsem.at[0])
    v_load = pltpu.make_async_copy(v_hbm.at[0], v_in, k_lsem.at[1])
    order_load = pltpu.make_async_copy(order_hbm, order_ref, k_lsem.at[2])
    plan_load = pltpu.make_async_copy(plan_hbm, plan_ref, k_lsem.at[3])
    plan_load.start()
    order_load.start()
    k_load.start()
    v_load.start()
    for i in range(chunks):
        q_load(i).start()

    barrier = pltpu.get_barrier_semaphore()

    @pl.loop(0, TP)
    def _(u):
        pl.semaphore_signal(barrier, inc=1, device_id={"section": after, "ctx": c, "tp": u}, device_id_type=MESH)
        pl.semaphore_signal(barrier, inc=1, device_id={"section": before, "ctx": c, "tp": u}, device_id_type=MESH)

    @pl.loop(1, NB)
    def _(o):
        b = lax.rem(me + o, NB)
        pl.semaphore_signal(barrier, inc=1, device_id={"section": s, "ctx": b // TP, "tp": lax.rem(b, TP)}, device_id_type=MESH)

    def do_copy(i):
        cols = pl.ds(pl.multiple_of(i * CW, CW), CW)
        return pltpu.make_async_remote_copy(
            src_ref=do_hbm.at[0, :, cols], dst_ref=do_got.at[i],
            send_sem=do_ssem.at[i], recv_sem=do_rsem.at[i],
            device_id={"section": before, "ctx": c, "tp": t}, device_id_type=MESH)

    def q_copy(i):
        return pltpu.make_async_remote_copy(
            src_ref=q_send.at[i], dst_ref=q_got.at[i],
            send_sem=q_ssem.at[i], recv_sem=q_rsem.at[i],
            device_id={"section": after, "ctx": c, "tp": t}, device_id_type=MESH)

    def kv_copy(u, b):
        return pltpu.make_async_remote_copy(
            src_ref=kv_send.at[u], dst_ref=kv_all.at[b],
            send_sem=kv_ssem.at[u], recv_sem=kv_rsem.at[b],
            device_id={"section": after, "ctx": c, "tp": u}, device_id_type=MESH)

    def kv_forward(b, u, to):
        return pltpu.make_async_remote_copy(
            src_ref=kv_all.at[b], dst_ref=kv_all.at[b],
            send_sem=fw_ssem.at[u, to], recv_sem=kv_rsem.at[b],
            device_id={"section": s, "ctx": to, "tp": t}, device_id_type=MESH)

    def g_copy(g, to, frm):
        return pltpu.make_async_remote_copy(
            src_ref=g_send.at[g, to], dst_ref=g_got.at[g, frm],
            send_sem=g_ssem.at[g, to], recv_sem=g_rsem.at[g, frm],
            device_id={"section": s, "ctx": to // TP, "tp": lax.rem(to, TP)}, device_id_type=MESH)

    plan_load.wait()
    slot = plan_ref[after]

    def picked(options):
        value = options[0]
        for m in range(1, len(options)):
            value = jnp.where(slot == m, options[m], value)
        return value

    def send_chunk(i):
        do_copy(i).start()
        q_load(i).wait()
        q_send[i] = picked([q_in[i, m] for m in range(q_in.shape[1])])
        q_copy(i).start()

    pl.semaphore_wait(barrier, 2 * TP + NB - 1)
    first = min(2, chunks)
    for i in range(first):
        send_chunk(i)

    k_load.wait()
    v_load.wait()
    for kind, src in enumerate((k_in, v_in)):
        rows = picked([src[:, m, :] for m in range(src.shape[1])])
        for u in range(TP):
            if KP != KR:
                kv_send[u, kind, KP - 16:, :] = jnp.zeros((16, W), BF16)
            kv_send[u, kind, :KR, :] = rows[:, u * W:(u + 1) * W]
    for o in range(TP):
        u = lax.rem(t + o, TP)
        kv_copy(u, me).start()
    for i in range(first, chunks):
        send_chunk(i)

    order_load.wait()

    col = lax.broadcasted_iota(jnp.int32, (1, KK), 1)
    blk = col // KP
    inner = col - blk * KP
    store_row = blk * KR + inner
    key_slot = store_row // block_len
    key_pos = store_row - key_slot * block_len
    for j in range(slots):
        key_pos = key_pos + jnp.where(key_slot == j, order_ref[j] * block_len, 0)
    key_pos = jnp.where(inner < KR, key_pos, jnp.int32(2**30))
    row = lax.broadcasted_iota(jnp.int32, (R, 1), 0)
    query_pos = row
    for j in range(R // block_len):
        base = order_ref[c * (R // block_len) + j] * block_len - j * block_len
        query_pos = query_pos + jnp.where(row // block_len == j, base, 0)
    bias[...] = jnp.where(key_pos <= query_pos, 0.0, NEG).astype(F32)

    for o in range(TP):
        u = lax.rem(t + TP - o, TP)
        b = c * TP + u
        kv_copy(t, b).wait_recv()

        @pl.loop(1, C)
        def _(k):
            kv_forward(b, u, lax.rem(c + k, C)).start()

    @pl.loop(TP, NB)
    def _(o):
        b = lax.rem(c * TP + o, NB)
        kv_copy(t, b).wait_recv()

    scale = hd ** -0.5
    scale2 = scale * math.log2(math.e)

    def out_copies(i):
        cols = pl.ds(pl.multiple_of(i * CW, CW), CW)
        return (
            pltpu.make_async_copy(attn_buf.at[i], attn_hbm.at[0, :, cols], out_sem.at[0, i]),
            pltpu.make_async_copy(dq_buf.at[i], dq_hbm.at[0, :, cols], out_sem.at[1, i]),
        )

    for g in range(kl):
        gc = slice(g * hd, (g + 1) * hd)
        dk_acc[...] = jnp.zeros_like(dk_acc)
        dv_acc[...] = jnp.zeros_like(dv_acc)

        @pl.loop(0, per_kv)
        def _(n):
            i = g * per_kv + n
            keys = kv_all[:, 0, :, gc].reshape(KK, hd)
            values = kv_all[:, 1, :, gc].reshape(KK, hd)
            q_copy(i).wait_recv()
            do_copy(i).wait_recv()
            for h in range(CH):
                hc = slice(h * hd, (h + 1) * hd)
                q = q_got[i, :, hc]
                do = do_got[i, :, hc]
                scores = nt_dot(q, keys) * scale2 + bias[...]
                top = jnp.max(scores, axis=1, keepdims=True)
                e = jnp.exp2(scores - top)
                total = jnp.sum(e, axis=1, keepdims=True)
                probs = e * (1.0 / total)
                low = probs.astype(BF16)
                attended = jnp.dot(low, values, preferred_element_type=F32)
                delta = jnp.sum(do.astype(F32) * attended, axis=1, keepdims=True)
                dprobs = nt_dot(do, values)
                ds = (probs * (dprobs - delta)).astype(BF16)
                attn_buf[i, :, hc] = attended.astype(BF16)
                dq_buf[i, :, hc] = (jnp.dot(ds, keys, preferred_element_type=F32) * scale).astype(BF16)
                dk_acc[...] += tn_dot(q, ds)
                dv_acc[...] += tn_dot(do, low)
            for copy in out_copies(i):
                copy.start()

        g_send[g, :, 0] = (dk_acc[...] * scale).T.astype(BF16).reshape(NB, KP, hd)
        g_send[g, :, 1] = dv_acc[...].T.astype(BF16).reshape(NB, KP, hd)

        @pl.loop(1, NB)
        def _(o):
            g_copy(g, lax.rem(me + o, NB), me).start()

        g_got[g, me] = g_send[g, me]

    for g in range(kl):
        @pl.loop(1, NB)
        def _(o):
            g_copy(g, me, lax.rem(me + o, NB)).wait_recv()

        for u in range(TP):
            cols = slice((u * kl + g) * hd, (u * kl + g + 1) * hd)
            for kind, out in enumerate((dk_out, dv_out)):
                total = g_got[g, u, kind].astype(F32)
                for cc in range(1, C):
                    total = total + g_got[g, cc * TP + u, kind].astype(F32)
                out[:, 0, cols] = total[:KR]
    dk_copy = pltpu.make_async_copy(dk_out, dk_hbm, grad_sem.at[0])
    dv_copy = pltpu.make_async_copy(dv_out, dv_hbm, grad_sem.at[1])
    dk_copy.start()
    dv_copy.start()

    @pl.loop(0, TP)
    def _(u):
        kv_copy(u, me).wait_send()

        @pl.loop(1, C)
        def _(k):
            kv_forward(c * TP + u, u, lax.rem(c + k, C)).wait_send()

    for g in range(kl):
        @pl.loop(1, NB)
        def _(o):
            g_copy(g, lax.rem(me + o, NB), me).wait_send()

    for i in range(chunks):
        q_copy(i).wait_send()
        do_copy(i).wait_send()
        for copy in out_copies(i):
            copy.wait()
    dk_copy.wait()
    dv_copy.wait()


def write_out(*refs):
    sems = refs[-1]
    copies = [pltpu.make_async_copy(refs[j], refs[4 + j], sems.at[j]) for j in range(4)]
    for copy in copies:
        copy.start()
    for copy in copies:
        copy.wait()


def solution(mesh):
    S, C, TP = mesh.shape["section"], mesh.shape["ctx"], mesh.shape["tp"]

    def body(block_order, plan, q_box, k_box, v_box, grad_out):
        hd = HEAD_DIM
        R, QC = q_box.shape[2:]
        KR, KW = k_box.shape[2:]
        block_len = R * C // block_order.shape[0]
        kl = KW // hd // TP
        group = QC // hd // kl
        CH = 2
        KP = -(-KR // 16) * 16
        NB = C * TP
        W = kl * hd
        CW = CH * hd
        chunks = QC // CW
        dims = (S, C, TP, R, KR, KP, kl, group, CH, block_len)
        dma = pltpu.SemaphoreType.DMA
        anywhere = pl.BlockSpec(memory_space=pl.ANY)
        hbm = pl.BlockSpec(memory_space=pltpu.HBM)
        results = pl.pallas_call(
            functools.partial(kernel, dims),
            out_shape=(
                pltpu.VMEM((1, R, QC), BF16),
                pltpu.VMEM((1, R, QC), BF16),
                pltpu.VMEM((KR, 1, KW), F32),
                pltpu.VMEM((KR, 1, KW), F32),
            ),
            in_specs=[hbm] * 6,
            out_specs=[anywhere] * 4,
            scratch_shapes=[
                pltpu.SMEM(block_order.shape, jnp.int32),
                pltpu.SMEM(plan.shape, jnp.int32),
                pltpu.VMEM((chunks, q_box.shape[1], R, CW), BF16),
                pltpu.VMEM((chunks, R, CW), BF16),
                pltpu.VMEM((chunks, R, CW), BF16),
                pltpu.VMEM((chunks, R, CW), BF16),
                pltpu.VMEM((KR, k_box.shape[1], KW), BF16),
                pltpu.VMEM((KR, k_box.shape[1], KW), BF16),
                pltpu.VMEM((TP, 2, KP, W), BF16),
                pltpu.VMEM((NB, 2, KP, W), BF16),
                pltpu.VMEM((R, NB * KP), F32),
                pltpu.VMEM((chunks, R, CW), BF16),
                pltpu.VMEM((chunks, R, CW), BF16),
                pltpu.VMEM((hd, NB * KP), F32),
                pltpu.VMEM((hd, NB * KP), F32),
                pltpu.VMEM((kl, NB, 2, KP, hd), BF16),
                pltpu.VMEM((kl, NB, 2, KP, hd), BF16),
                pltpu.VMEM((KR, 1, KW), F32),
                pltpu.VMEM((KR, 1, KW), F32),
                dma((chunks,)), dma((4,)), dma((chunks,)), dma((chunks,)), dma((chunks,)), dma((chunks,)),
                dma((TP,)), dma((NB,)), dma((TP, C)), dma((kl, NB)), dma((kl, NB)), dma((2, chunks)), dma((2,)),
            ],
            compiler_params=pltpu.CompilerParams(
                collective_id=0, has_side_effects=True, vmem_limit_bytes=56 * 1024 * 1024
            ),
        )(block_order, plan, q_box, k_box.transpose(0, 2, 1, 3), v_box.transpose(0, 2, 1, 3), grad_out)
        attn, dq, dk, dv = pl.pallas_call(
            write_out,
            out_shape=tuple(jax.ShapeDtypeStruct(r.shape, r.dtype) for r in results),
            in_specs=[anywhere] * 4,
            out_specs=[hbm] * 4,
            scratch_shapes=[dma((4,))],
            compiler_params=pltpu.CompilerParams(vmem_limit_bytes=8 * 1024 * 1024),
        )(*results)
        return attn, dq, dk.transpose(1, 0, 2), dv.transpose(1, 0, 2)

    in_specs = (
        P(),
        P(),
        P("section", None, "ctx", "tp"),
        P("section", None, ("ctx", "tp"), None),
        P("section", None, ("ctx", "tp"), None),
        P("section", "ctx", "tp"),
    )
    out_specs = (
        P("section", "ctx", "tp"),
        P("section", "ctx", "tp"),
        P("section", ("ctx", "tp"), None),
        P("section", ("ctx", "tp"), None),
    )
    return jax.shard_map(body, mesh=mesh, in_specs=in_specs, out_specs=out_specs, check_vma=False)
```

```python
import functools
import math

import jax
import jax.numpy as jnp
from jax import lax
from jax.experimental import pallas as pl
from jax.experimental.pallas import tpu as pltpu
from jax.sharding import PartitionSpec as P

HEAD_DIM = 128
NEG = -1e30
MESH = pl.DeviceIdType.MESH
F32 = jnp.float32
BF16 = jnp.bfloat16


def nt_dot(a, b):
    return lax.dot_general(a, b, (((1,), (1,)), ((), ())), preferred_element_type=F32)


def tn_dot(a, b):
    return lax.dot_general(a, b, (((0,), (0,)), ((), ())), preferred_element_type=F32)


def kernel(
    dims,
    order_hbm, plan_hbm, q_hbm, k_hbm, v_hbm, do_hbm,
    attn_hbm, dq_hbm, dk_hbm, dv_hbm,
    order_ref, plan_ref, q_in, q_send, q_got, do_got, k_in, v_in, kv_send, kv_all, bias,
    attn_buf, dq_buf, dk_acc, dv_acc, g_send, g_got, dk_out, dv_out,
    q_lsem, k_lsem, q_ssem, q_rsem, do_ssem, do_rsem, kv_ssem, kv_rsem, fw_ssem,
    g_ssem, g_rsem, out_sem, grad_sem,
):
    S, C, TP, R, KR, KP, kl, group, CH, block_len = dims
    hd = HEAD_DIM
    W = kl * hd
    NB = C * TP
    KK = NB * KP
    CW = CH * hd
    per_kv = group // CH
    chunks = kl * per_kv
    slots = NB * KR // block_len
    s, c, t = lax.axis_index("section"), lax.axis_index("ctx"), lax.axis_index("tp")
    me = c * TP + t
    after, before = lax.rem(s + 1, S), lax.rem(s + S - 1, S)

    def q_load(i):
        cols = pl.ds(pl.multiple_of(i * CW, CW), CW)
        return pltpu.make_async_copy(q_hbm.at[0, :, :, cols], q_in.at[i], q_lsem.at[i])

    k_load = pltpu.make_async_copy(k_hbm.at[0], k_in, k_lsem.at[0])
    v_load = pltpu.make_async_copy(v_hbm.at[0], v_in, k_lsem.at[1])
    order_load = pltpu.make_async_copy(order_hbm, order_ref, k_lsem.at[2])
    plan_load = pltpu.make_async_copy(plan_hbm, plan_ref, k_lsem.at[3])
    plan_load.start()
    order_load.start()
    k_load.start()
    v_load.start()
    for i in range(chunks):
        q_load(i).start()

    barrier = pltpu.get_barrier_semaphore()

    @pl.loop(0, TP)
    def _(u):
        pl.semaphore_signal(barrier, inc=1, device_id={"section": after, "ctx": c, "tp": u}, device_id_type=MESH)
        pl.semaphore_signal(barrier, inc=1, device_id={"section": before, "ctx": c, "tp": u}, device_id_type=MESH)

    @pl.loop(1, NB)
    def _(o):
        b = lax.rem(me + o, NB)
        pl.semaphore_signal(barrier, inc=1, device_id={"section": s, "ctx": b // TP, "tp": lax.rem(b, TP)}, device_id_type=MESH)

    def do_copy(i):
        cols = pl.ds(pl.multiple_of(i * CW, CW), CW)
        return pltpu.make_async_remote_copy(
            src_ref=do_hbm.at[0, :, cols], dst_ref=do_got.at[i],
            send_sem=do_ssem.at[i], recv_sem=do_rsem.at[i],
            device_id={"section": before, "ctx": c, "tp": t}, device_id_type=MESH)

    def q_copy(i):
        return pltpu.make_async_remote_copy(
            src_ref=q_send.at[i], dst_ref=q_got.at[i],
            send_sem=q_ssem.at[i], recv_sem=q_rsem.at[i],
            device_id={"section": after, "ctx": c, "tp": t}, device_id_type=MESH)

    def kv_copy(u, b):
        return pltpu.make_async_remote_copy(
            src_ref=kv_send.at[u], dst_ref=kv_all.at[b],
            send_sem=kv_ssem.at[u], recv_sem=kv_rsem.at[b],
            device_id={"section": after, "ctx": c, "tp": u}, device_id_type=MESH)

    def kv_forward(b, u, to):
        return pltpu.make_async_remote_copy(
            src_ref=kv_all.at[b], dst_ref=kv_all.at[b],
            send_sem=fw_ssem.at[u, to], recv_sem=kv_rsem.at[b],
            device_id={"section": s, "ctx": to, "tp": t}, device_id_type=MESH)

    def g_copy(g, to, frm):
        return pltpu.make_async_remote_copy(
            src_ref=g_send.at[g, to], dst_ref=g_got.at[g, frm],
            send_sem=g_ssem.at[g, to], recv_sem=g_rsem.at[g, frm],
            device_id={"section": s, "ctx": to // TP, "tp": lax.rem(to, TP)}, device_id_type=MESH)

    plan_load.wait()
    slot = plan_ref[after]

    def picked(options):
        value = options[0]
        for m in range(1, len(options)):
            value = jnp.where(slot == m, options[m], value)
        return value

    def send_chunk(i):
        do_copy(i).start()
        q_load(i).wait()
        q_send[i] = picked([q_in[i, m] for m in range(q_in.shape[1])])
        q_copy(i).start()

    pl.semaphore_wait(barrier, 2 * TP + NB - 1)
    first = min(4, chunks)
    for i in range(first):
        send_chunk(i)

    k_load.wait()
    v_load.wait()
    for kind, src in enumerate((k_in, v_in)):
        rows = picked([src[:, m, :] for m in range(src.shape[1])])
        for u in range(TP):
            if KP != KR:
                kv_send[u, kind, KP - 16:, :] = jnp.zeros((16, W), BF16)
            kv_send[u, kind, :KR, :] = rows[:, u * W:(u + 1) * W]
    for o in range(TP):
        u = lax.rem(t + o, TP)
        kv_copy(u, me).start()
    for i in range(first, chunks):
        send_chunk(i)

    order_load.wait()

    col = lax.broadcasted_iota(jnp.int32, (1, KK), 1)
    blk = col // KP
    inner = col - blk * KP
    store_row = blk * KR + inner
    key_slot = store_row // block_len
    key_pos = store_row - key_slot * block_len
    for j in range(slots):
        key_pos = key_pos + jnp.where(key_slot == j, order_ref[j] * block_len, 0)
    key_pos = jnp.where(inner < KR, key_pos, jnp.int32(2**30))
    row = lax.broadcasted_iota(jnp.int32, (R, 1), 0)
    query_pos = row
    for j in range(R // block_len):
        base = order_ref[c * (R // block_len) + j] * block_len - j * block_len
        query_pos = query_pos + jnp.where(row // block_len == j, base, 0)
    bias[...] = jnp.where(key_pos <= query_pos, 0.0, NEG).astype(F32)

    for o in range(TP):
        u = lax.rem(t + TP - o, TP)
        b = c * TP + u
        kv_copy(t, b).wait_recv()

        @pl.loop(1, C)
        def _(k):
            kv_forward(b, u, lax.rem(c + k, C)).start()

    @pl.loop(TP, NB)
    def _(o):
        b = lax.rem(c * TP + o, NB)
        kv_copy(t, b).wait_recv()

    scale = hd ** -0.5
    scale2 = scale * math.log2(math.e)

    def out_copies(i):
        cols = pl.ds(pl.multiple_of(i * CW, CW), CW)
        return (
            pltpu.make_async_copy(attn_buf.at[i], attn_hbm.at[0, :, cols], out_sem.at[0, i]),
            pltpu.make_async_copy(dq_buf.at[i], dq_hbm.at[0, :, cols], out_sem.at[1, i]),
        )

    for g in range(kl):
        gc = slice(g * hd, (g + 1) * hd)
        dk_acc[...] = jnp.zeros_like(dk_acc)
        dv_acc[...] = jnp.zeros_like(dv_acc)

        @pl.loop(0, per_kv)
        def _(n):
            i = g * per_kv + n
            keys = kv_all[:, 0, :, gc].reshape(KK, hd)
            values = kv_all[:, 1, :, gc].reshape(KK, hd)
            q_copy(i).wait_recv()
            do_copy(i).wait_recv()
            for h in range(CH):
                hc = slice(h * hd, (h + 1) * hd)
                q = q_got[i, :, hc]
                do = do_got[i, :, hc]
                scores = nt_dot(q, keys) * scale2 + bias[...]
                top = jnp.max(scores, axis=1, keepdims=True)
                e = jnp.exp2(scores - top)
                total = jnp.sum(e, axis=1, keepdims=True)
                probs = e * (1.0 / total)
                low = probs.astype(BF16)
                attended = jnp.dot(low, values, preferred_element_type=F32)
                delta = jnp.sum(do.astype(F32) * attended, axis=1, keepdims=True)
                dprobs = nt_dot(do, values)
                ds = (probs * (dprobs - delta)).astype(BF16)
                attn_buf[i, :, hc] = attended.astype(BF16)
                dq_buf[i, :, hc] = (jnp.dot(ds, keys, preferred_element_type=F32) * scale).astype(BF16)
                dk_acc[...] += tn_dot(q, ds)
                dv_acc[...] += tn_dot(do, low)
            for copy in out_copies(i):
                copy.start()

        g_send[g, :, 0] = (dk_acc[...] * scale).astype(BF16).T.reshape(NB, KP, hd)
        g_send[g, :, 1] = dv_acc[...].astype(BF16).T.reshape(NB, KP, hd)

        @pl.loop(1, NB)
        def _(o):
            g_copy(g, lax.rem(me + o, NB), me).start()

        g_got[g, me] = g_send[g, me]

    for g in range(kl):
        @pl.loop(1, NB)
        def _(o):
            g_copy(g, me, lax.rem(me + o, NB)).wait_recv()

        for u in range(TP):
            cols = slice((u * kl + g) * hd, (u * kl + g + 1) * hd)
            for kind, out in enumerate((dk_out, dv_out)):
                total = g_got[g, u, kind].astype(F32)
                for cc in range(1, C):
                    total = total + g_got[g, cc * TP + u, kind].astype(F32)
                out[:, 0, cols] = total[:KR]
    dk_copy = pltpu.make_async_copy(dk_out, dk_hbm, grad_sem.at[0])
    dv_copy = pltpu.make_async_copy(dv_out, dv_hbm, grad_sem.at[1])
    dk_copy.start()
    dv_copy.start()

    @pl.loop(0, TP)
    def _(u):
        kv_copy(u, me).wait_send()

        @pl.loop(1, C)
        def _(k):
            kv_forward(c * TP + u, u, lax.rem(c + k, C)).wait_send()

    for g in range(kl):
        @pl.loop(1, NB)
        def _(o):
            g_copy(g, lax.rem(me + o, NB), me).wait_send()

    for i in range(chunks):
        q_copy(i).wait_send()
        do_copy(i).wait_send()
        for copy in out_copies(i):
            copy.wait()
    dk_copy.wait()
    dv_copy.wait()


def write_out(*refs):
    sems = refs[-1]
    copies = [pltpu.make_async_copy(refs[j], refs[4 + j], sems.at[j]) for j in range(4)]
    for copy in copies:
        copy.start()
    for copy in copies:
        copy.wait()


def solution(mesh):
    S, C, TP = mesh.shape["section"], mesh.shape["ctx"], mesh.shape["tp"]

    def body(block_order, plan, q_box, k_box, v_box, grad_out):
        hd = HEAD_DIM
        R, QC = q_box.shape[2:]
        KR, KW = k_box.shape[2:]
        block_len = R * C // block_order.shape[0]
        kl = KW // hd // TP
        group = QC // hd // kl
        CH = 1
        KP = -(-KR // 16) * 16
        NB = C * TP
        W = kl * hd
        CW = CH * hd
        chunks = QC // CW
        dims = (S, C, TP, R, KR, KP, kl, group, CH, block_len)
        dma = pltpu.SemaphoreType.DMA
        anywhere = pl.BlockSpec(memory_space=pl.ANY)
        hbm = pl.BlockSpec(memory_space=pltpu.HBM)
        results = pl.pallas_call(
            functools.partial(kernel, dims),
            out_shape=(
                pltpu.VMEM((1, R, QC), BF16),
                pltpu.VMEM((1, R, QC), BF16),
                pltpu.VMEM((KR, 1, KW), F32),
                pltpu.VMEM((KR, 1, KW), F32),
            ),
            in_specs=[hbm] * 6,
            out_specs=[anywhere] * 4,
            scratch_shapes=[
                pltpu.SMEM(block_order.shape, jnp.int32),
                pltpu.SMEM(plan.shape, jnp.int32),
                pltpu.VMEM((chunks, q_box.shape[1], R, CW), BF16),
                pltpu.VMEM((chunks, R, CW), BF16),
                pltpu.VMEM((chunks, R, CW), BF16),
                pltpu.VMEM((chunks, R, CW), BF16),
                pltpu.VMEM((KR, k_box.shape[1], KW), BF16),
                pltpu.VMEM((KR, k_box.shape[1], KW), BF16),
                pltpu.VMEM((TP, 2, KP, W), BF16),
                pltpu.VMEM((NB, 2, KP, W), BF16),
                pltpu.VMEM((R, NB * KP), F32),
                pltpu.VMEM((chunks, R, CW), BF16),
                pltpu.VMEM((chunks, R, CW), BF16),
                pltpu.VMEM((hd, NB * KP), F32),
                pltpu.VMEM((hd, NB * KP), F32),
                pltpu.VMEM((kl, NB, 2, KP, hd), BF16),
                pltpu.VMEM((kl, NB, 2, KP, hd), BF16),
                pltpu.VMEM((KR, 1, KW), F32),
                pltpu.VMEM((KR, 1, KW), F32),
                dma((chunks,)), dma((4,)), dma((chunks,)), dma((chunks,)), dma((chunks,)), dma((chunks,)),
                dma((TP,)), dma((NB,)), dma((TP, C)), dma((kl, NB)), dma((kl, NB)), dma((2, chunks)), dma((2,)),
            ],
            compiler_params=pltpu.CompilerParams(
                collective_id=0, has_side_effects=True, vmem_limit_bytes=56 * 1024 * 1024
            ),
        )(block_order, plan, q_box, k_box.transpose(0, 2, 1, 3), v_box.transpose(0, 2, 1, 3), grad_out)
        attn, dq, dk, dv = pl.pallas_call(
            write_out,
            out_shape=tuple(jax.ShapeDtypeStruct(r.shape, r.dtype) for r in results),
            in_specs=[anywhere] * 4,
            out_specs=[hbm] * 4,
            scratch_shapes=[dma((4,))],
            compiler_params=pltpu.CompilerParams(vmem_limit_bytes=8 * 1024 * 1024),
        )(*results)
        return attn, dq, dk.transpose(1, 0, 2), dv.transpose(1, 0, 2)

    in_specs = (
        P(),
        P(),
        P("section", None, "ctx", "tp"),
        P("section", None, ("ctx", "tp"), None),
        P("section", None, ("ctx", "tp"), None),
        P("section", "ctx", "tp"),
    )
    out_specs = (
        P("section", "ctx", "tp"),
        P("section", "ctx", "tp"),
        P("section", ("ctx", "tp"), None),
        P("section", ("ctx", "tp"), None),
    )
    return jax.shard_map(body, mesh=mesh, in_specs=in_specs, out_specs=out_specs, check_vma=False)
```

```python
import functools
import math

import jax
import jax.numpy as jnp
from jax import lax
from jax.experimental import pallas as pl
from jax.experimental.pallas import tpu as pltpu
from jax.sharding import PartitionSpec as P

HEAD_DIM = 128
NEG = -1e30
MESH = pl.DeviceIdType.MESH
F32 = jnp.float32
BF16 = jnp.bfloat16


def nt_dot(a, b):
    return lax.dot_general(a, b, (((1,), (1,)), ((), ())), preferred_element_type=F32)


def tn_dot(a, b):
    return lax.dot_general(a, b, (((0,), (0,)), ((), ())), preferred_element_type=F32)


def kernel(
    dims,
    order_hbm, plan_hbm, q_hbm, k_hbm, v_hbm, do_hbm,
    attn_hbm, dq_hbm, dk_out, dv_out,
    order_ref, plan_ref, q_in, q_send, q_got, do_got, k_in, v_in, kv_send, kv_all, bias,
    attn_buf, dq_buf, dk_acc, dv_acc, g_send, g_got,
    q_lsem, k_lsem, q_ssem, q_rsem, do_ssem, do_rsem, kv_ssem, kv_rsem, fw_ssem,
    g_ssem, g_rsem, out_sem,
):
    S, C, TP, R, KR, KP, kl, group, CH, block_len = dims
    hd = HEAD_DIM
    W = kl * hd
    NB = C * TP
    KK = NB * KP
    CW = CH * hd
    per_kv = group // CH
    chunks = kl * per_kv
    slots = NB * KR // block_len
    s, c, t = lax.axis_index("section"), lax.axis_index("ctx"), lax.axis_index("tp")
    me = c * TP + t
    after, before = lax.rem(s + 1, S), lax.rem(s + S - 1, S)

    def q_load(i):
        cols = pl.ds(pl.multiple_of(i * CW, CW), CW)
        return pltpu.make_async_copy(q_hbm.at[0, :, :, cols], q_in.at[i], q_lsem.at[i])

    k_load = pltpu.make_async_copy(k_hbm.at[0], k_in, k_lsem.at[0])
    v_load = pltpu.make_async_copy(v_hbm.at[0], v_in, k_lsem.at[1])
    order_load = pltpu.make_async_copy(order_hbm, order_ref, k_lsem.at[2])
    plan_load = pltpu.make_async_copy(plan_hbm, plan_ref, k_lsem.at[3])
    plan_load.start()
    order_load.start()
    k_load.start()
    v_load.start()
    for i in range(chunks):
        q_load(i).start()

    barrier = pltpu.get_barrier_semaphore()

    @pl.loop(0, TP)
    def _(u):
        pl.semaphore_signal(barrier, inc=1, device_id={"section": after, "ctx": c, "tp": u}, device_id_type=MESH)
        pl.semaphore_signal(barrier, inc=1, device_id={"section": before, "ctx": c, "tp": u}, device_id_type=MESH)

    @pl.loop(1, NB)
    def _(o):
        b = lax.rem(me + o, NB)
        pl.semaphore_signal(barrier, inc=1, device_id={"section": s, "ctx": b // TP, "tp": lax.rem(b, TP)}, device_id_type=MESH)

    def do_copy(i):
        cols = pl.ds(pl.multiple_of(i * CW, CW), CW)
        return pltpu.make_async_remote_copy(
            src_ref=do_hbm.at[0, :, cols], dst_ref=do_got.at[i],
            send_sem=do_ssem.at[i], recv_sem=do_rsem.at[i],
            device_id={"section": before, "ctx": c, "tp": t}, device_id_type=MESH)

    def q_copy(i):
        return pltpu.make_async_remote_copy(
            src_ref=q_send.at[i], dst_ref=q_got.at[i],
            send_sem=q_ssem.at[i], recv_sem=q_rsem.at[i],
            device_id={"section": after, "ctx": c, "tp": t}, device_id_type=MESH)

    def kv_copy(u, b):
        return pltpu.make_async_remote_copy(
            src_ref=kv_send.at[u], dst_ref=kv_all.at[b],
            send_sem=kv_ssem.at[u], recv_sem=kv_rsem.at[b],
            device_id={"section": after, "ctx": c, "tp": u}, device_id_type=MESH)

    def kv_forward(b, u, to):
        return pltpu.make_async_remote_copy(
            src_ref=kv_all.at[b], dst_ref=kv_all.at[b],
            send_sem=fw_ssem.at[u, to], recv_sem=kv_rsem.at[b],
            device_id={"section": s, "ctx": to, "tp": t}, device_id_type=MESH)

    def g_copy(g, to, frm):
        return pltpu.make_async_remote_copy(
            src_ref=g_send.at[g, to], dst_ref=g_got.at[g, frm],
            send_sem=g_ssem.at[g, to], recv_sem=g_rsem.at[g, frm],
            device_id={"section": s, "ctx": to // TP, "tp": lax.rem(to, TP)}, device_id_type=MESH)

    plan_load.wait()
    slot = plan_ref[after]

    def picked(options):
        value = options[0]
        for m in range(1, len(options)):
            value = jnp.where(slot == m, options[m], value)
        return value

    def send_chunk(i):
        do_copy(i).start()
        q_load(i).wait()
        q_send[i] = picked([q_in[i, m] for m in range(q_in.shape[1])])
        q_copy(i).start()

    pl.semaphore_wait(barrier, 2 * TP + NB - 1)
    first = min(4, chunks)
    for i in range(first):
        send_chunk(i)

    k_load.wait()
    v_load.wait()
    for kind, src in enumerate((k_in, v_in)):
        rows = picked([src[:, m, :] for m in range(src.shape[1])])
        for u in range(TP):
            if KP != KR:
                kv_send[u, kind, KP - 16:, :] = jnp.zeros((16, W), BF16)
            kv_send[u, kind, :KR, :] = rows[:, u * W:(u + 1) * W]
    for o in range(TP):
        u = lax.rem(t + o, TP)
        kv_copy(u, me).start()
    for i in range(first, chunks):
        send_chunk(i)

    order_load.wait()

    col = lax.broadcasted_iota(jnp.int32, (1, KK), 1)
    blk = col // KP
    inner = col - blk * KP
    store_row = blk * KR + inner
    key_slot = store_row // block_len
    key_pos = store_row - key_slot * block_len
    for j in range(slots):
        key_pos = key_pos + jnp.where(key_slot == j, order_ref[j] * block_len, 0)
    key_pos = jnp.where(inner < KR, key_pos, jnp.int32(2**30))
    row = lax.broadcasted_iota(jnp.int32, (R, 1), 0)
    query_pos = row
    for j in range(R // block_len):
        base = order_ref[c * (R // block_len) + j] * block_len - j * block_len
        query_pos = query_pos + jnp.where(row // block_len == j, base, 0)
    bias[...] = jnp.where(key_pos <= query_pos, 0.0, NEG).astype(F32)

    for o in range(TP):
        u = lax.rem(t + TP - o, TP)
        b = c * TP + u
        kv_copy(t, b).wait_recv()

        @pl.loop(1, C)
        def _(k):
            kv_forward(b, u, lax.rem(c + k, C)).start()

    @pl.loop(TP, NB)
    def _(o):
        b = lax.rem(c * TP + o, NB)
        kv_copy(t, b).wait_recv()

    scale = hd ** -0.5
    scale2 = scale * math.log2(math.e)

    def out_copies(i):
        cols = pl.ds(pl.multiple_of(i * CW, CW), CW)
        return (
            pltpu.make_async_copy(attn_buf.at[i], attn_hbm.at[0, :, cols], out_sem.at[0, i]),
            pltpu.make_async_copy(dq_buf.at[i], dq_hbm.at[0, :, cols], out_sem.at[1, i]),
        )

    for g in range(kl):
        gc = slice(g * hd, (g + 1) * hd)
        dk_acc[...] = jnp.zeros_like(dk_acc)
        dv_acc[...] = jnp.zeros_like(dv_acc)

        @pl.loop(0, per_kv)
        def _(n):
            i = g * per_kv + n
            keys = kv_all[:, 0, :, gc].reshape(KK, hd)
            values = kv_all[:, 1, :, gc].reshape(KK, hd)
            q_copy(i).wait_recv()
            do_copy(i).wait_recv()
            for h in range(CH):
                hc = slice(h * hd, (h + 1) * hd)
                q = q_got[i, :, hc]
                do = do_got[i, :, hc]
                scores = nt_dot(q, keys) * scale2 + bias[...]
                top = jnp.max(scores, axis=1, keepdims=True)
                e = jnp.exp2(scores - top)
                total = jnp.sum(e, axis=1, keepdims=True)
                probs = e * (1.0 / total)
                low = probs.astype(BF16)
                attended = jnp.dot(low, values, preferred_element_type=F32)
                delta = jnp.sum(do.astype(F32) * attended, axis=1, keepdims=True)
                dprobs = nt_dot(do, values)
                ds = (probs * (dprobs - delta)).astype(BF16)
                attn_buf[i, :, hc] = attended.astype(BF16)
                dq_buf[i, :, hc] = (jnp.dot(ds, keys, preferred_element_type=F32) * scale).astype(BF16)
                dk_acc[...] += tn_dot(q, ds)
                dv_acc[...] += tn_dot(do, low)
            for copy in out_copies(i):
                copy.start()

        g_send[g, :, 0] = (dk_acc[...] * scale).astype(BF16).T.reshape(NB, KP, hd)
        g_send[g, :, 1] = dv_acc[...].astype(BF16).T.reshape(NB, KP, hd)

        @pl.loop(1, NB)
        def _(o):
            g_copy(g, lax.rem(me + o, NB), me).start()

        g_got[g, me] = g_send[g, me]

    for g in range(kl):
        @pl.loop(1, NB)
        def _(o):
            g_copy(g, me, lax.rem(me + o, NB)).wait_recv()

        for u in range(TP):
            cols = slice((u * kl + g) * hd, (u * kl + g + 1) * hd)
            for kind, out in enumerate((dk_out, dv_out)):
                total = g_got[g, u, kind].astype(F32)
                for cc in range(1, C):
                    total = total + g_got[g, cc * TP + u, kind].astype(F32)
                out[:, 0, cols] = total[:KR]

    @pl.loop(0, TP)
    def _(u):
        kv_copy(u, me).wait_send()

        @pl.loop(1, C)
        def _(k):
            kv_forward(c * TP + u, u, lax.rem(c + k, C)).wait_send()

    for g in range(kl):
        @pl.loop(1, NB)
        def _(o):
            g_copy(g, lax.rem(me + o, NB), me).wait_send()

    for i in range(chunks):
        q_copy(i).wait_send()
        do_copy(i).wait_send()
        for copy in out_copies(i):
            copy.wait()


def write_out(*refs):
    sems = refs[-1]
    copies = [pltpu.make_async_copy(refs[j], refs[4 + j], sems.at[j]) for j in range(4)]
    for copy in copies:
        copy.start()
    for copy in copies:
        copy.wait()


def solution(mesh):
    S, C, TP = mesh.shape["section"], mesh.shape["ctx"], mesh.shape["tp"]

    def body(block_order, plan, q_box, k_box, v_box, grad_out):
        hd = HEAD_DIM
        R, QC = q_box.shape[2:]
        KR, KW = k_box.shape[2:]
        block_len = R * C // block_order.shape[0]
        kl = KW // hd // TP
        group = QC // hd // kl
        CH = 1
        KP = -(-KR // 16) * 16
        NB = C * TP
        W = kl * hd
        CW = CH * hd
        chunks = QC // CW
        dims = (S, C, TP, R, KR, KP, kl, group, CH, block_len)
        dma = pltpu.SemaphoreType.DMA
        anywhere = pl.BlockSpec(memory_space=pl.ANY)
        hbm = pl.BlockSpec(memory_space=pltpu.HBM)
        results = pl.pallas_call(
            functools.partial(kernel, dims),
            out_shape=(
                pltpu.VMEM((1, R, QC), BF16),
                pltpu.VMEM((1, R, QC), BF16),
                pltpu.VMEM((KR, 1, KW), F32),
                pltpu.VMEM((KR, 1, KW), F32),
            ),
            in_specs=[hbm] * 6,
            out_specs=[anywhere] * 2 + [pl.BlockSpec(memory_space=pltpu.VMEM)] * 2,
            scratch_shapes=[
                pltpu.SMEM(block_order.shape, jnp.int32),
                pltpu.SMEM(plan.shape, jnp.int32),
                pltpu.VMEM((chunks, q_box.shape[1], R, CW), BF16),
                pltpu.VMEM((chunks, R, CW), BF16),
                pltpu.VMEM((chunks, R, CW), BF16),
                pltpu.VMEM((chunks, R, CW), BF16),
                pltpu.VMEM((KR, k_box.shape[1], KW), BF16),
                pltpu.VMEM((KR, k_box.shape[1], KW), BF16),
                pltpu.VMEM((TP, 2, KP, W), BF16),
                pltpu.VMEM((NB, 2, KP, W), BF16),
                pltpu.VMEM((R, NB * KP), F32),
                pltpu.VMEM((chunks, R, CW), BF16),
                pltpu.VMEM((chunks, R, CW), BF16),
                pltpu.VMEM((hd, NB * KP), F32),
                pltpu.VMEM((hd, NB * KP), F32),
                pltpu.VMEM((kl, NB, 2, KP, hd), BF16),
                pltpu.VMEM((kl, NB, 2, KP, hd), BF16),
                dma((chunks,)), dma((4,)), dma((chunks,)), dma((chunks,)), dma((chunks,)), dma((chunks,)),
                dma((TP,)), dma((NB,)), dma((TP, C)), dma((kl, NB)), dma((kl, NB)), dma((2, chunks)),
            ],
            compiler_params=pltpu.CompilerParams(
                collective_id=0, has_side_effects=True, vmem_limit_bytes=56 * 1024 * 1024
            ),
        )(block_order, plan, q_box, k_box.transpose(0, 2, 1, 3), v_box.transpose(0, 2, 1, 3), grad_out)
        attn, dq, dk, dv = pl.pallas_call(
            write_out,
            out_shape=tuple(jax.ShapeDtypeStruct(r.shape, r.dtype) for r in results),
            in_specs=[anywhere] * 4,
            out_specs=[hbm] * 4,
            scratch_shapes=[dma((4,))],
            compiler_params=pltpu.CompilerParams(vmem_limit_bytes=8 * 1024 * 1024),
        )(*results)
        return attn, dq, dk.transpose(1, 0, 2), dv.transpose(1, 0, 2)

    in_specs = (
        P(),
        P(),
        P("section", None, "ctx", "tp"),
        P("section", None, ("ctx", "tp"), None),
        P("section", None, ("ctx", "tp"), None),
        P("section", "ctx", "tp"),
    )
    out_specs = (
        P("section", "ctx", "tp"),
        P("section", "ctx", "tp"),
        P("section", ("ctx", "tp"), None),
        P("section", ("ctx", "tp"), None),
    )
    return jax.shard_map(body, mesh=mesh, in_specs=in_specs, out_specs=out_specs, check_vma=False)
```
